256 devices in a mesh: dp: 4 (over x_lo, core), center: 64 (over y, x_hi, z).
Axes of the slice: x: 4 (x_hi: 2, x_lo: 2; x = x_hi * 2 + x_lo), y: 4, z: 8, core: 2. Of those that a mesh axis runs over, the one named last changes fastest.
Arguments:
- centers: bfloat16 [131072, 768], P('center'), may hold values from -0.5 to 0.5
- weights: float32 [131072, 256], P('center'), may hold values from -0.0625 to 0.0625
- batch_index: int32 [1024], P('dp'), may hold values from 0 to 131071
- targets: float32 [1024, 256], P('dp'), may hold values from -6 to 6
- subset_points: bfloat16 [2048, 768], P('center'), may hold values from -0.5 to 0.5
- eigvecs: float32 [2048, 200], P('center'), may hold values from -0.125 to 0.125
- shrink: float32 [200], replicated, may hold values from 0.05 to 0.95
Outputs:
- step: float32 [131072, 256], P('center')
The draws below stay inside these ranges and needn't reach their ends.
All inputs are finite; a program needn't handle non-finite values.
Results may differ from the reference program's by a relative error of at most 0.0003.
Values may be sent and summed in bfloat16 or wider, within the bound.
A program may use at most 128 MiB of HBM per device.

```python
import math
import jax
import jax.numpy as jnp
from jax import lax

D = 768
OUTS = 256
Q = 200
P_DEV = 2048
CENTERS = 131072
BATCH = 1024
SUBSET = 2048
N_CENTER = 64


def cluster_layout(key, low, high):
    count = BATCH // 8
    means = jnp.clip(jax.random.normal(key, (count, D), jnp.float32), -4.0, 4.0)
    level = jax.random.uniform(jax.random.fold_in(key, 101), (count, 1), jnp.float32)
    return means * (low * jnp.exp(level * jnp.log(high / low)))


def place_rows(layout, key, noise, low, high):
    total_rows = noise.shape[0]
    owner = jax.random.randint(jax.random.fold_in(key, 7), (total_rows,), 0, layout.shape[0])
    level = jax.random.uniform(jax.random.fold_in(key, 8), (total_rows, 1), jnp.float32)
    spread = low * jnp.exp(level * jnp.log(high / low))
    return jnp.clip(layout[owner] + spread * noise, -0.5, 0.5).astype(jnp.bfloat16)


def draw_centers(key, part):
    layout = cluster_layout(key, 0.03, 0.08)
    key = jax.random.fold_in(key, 3)
    noise = jnp.clip(jax.random.normal(jax.random.fold_in(key, 9), (CENTERS, D), jnp.float32), -4.0, 4.0)
    return place_rows(layout, key, noise, 0.004, 0.03)


def draw_subset_points(key, part):
    layout = cluster_layout(key, 0.03, 0.08)
    key = jax.random.fold_in(key, 5)
    noise = jnp.clip(jax.random.normal(jax.random.fold_in(key, 9), (SUBSET, D), jnp.float32), -4.0, 4.0)
    return place_rows(layout, key, noise, 0.004, 0.03)


def place_ends(values, stream_key, smallest, high):
    longest = values.shape.index(max(values.shape))
    spots = []
    for shift in (0, 1):
        where = [jax.random.randint(jax.random.fold_in(stream_key, axis), (), 0, length) for axis, length in enumerate(values.shape)]
        where[longest] = (where[longest] + shift) % values.shape[longest]
        spots.append(tuple(where))
    return values.at[spots[0]].set(smallest).at[spots[1]].set(high)


def levels(key, shape, pieces, least, top_value):
    gain = 1.0
    for dim, shards_of in pieces:
        draws = jax.random.uniform(jax.random.fold_in(jax.random.fold_in(key, 6), dim), (shards_of,), jnp.float32, least / len(pieces), top_value / len(pieces))
        gain = gain * jnp.repeat(jnp.exp(draws), shape[dim] // shards_of).reshape((-1,) + (1,) * (len(shape) - 1 - dim))
    return gain


def scatter_about(key, extent, deviation, bound, split=(), kind=jnp.bfloat16):
    values = jax.random.normal(key, extent, jnp.float32) * deviation
    if len(split) > 0:
        values = levels(key, extent, split, -0.22, 0.18) * values
    return jnp.clip(values, min=-bound, max=bound).astype(kind)


def setup_inputs(seed: int = 0) -> dict:
    splits = jax.random.split(jax.random.key(seed), 8)
    centers = draw_centers(jax.random.fold_in(splits[7], 71), 0)
    weights = scatter_about(splits[1], (CENTERS, OUTS), (CENTERS // 16) ** -0.5, 0.0625, ((0, 64),), jnp.float32)
    batch_index = place_ends(jax.random.randint(splits[2], (BATCH,), 0, CENTERS), jax.random.fold_in(splits[2], 1), 0, CENTERS - 1).astype(jnp.int32)
    targets = scatter_about(splits[3], (BATCH, OUTS), 1.0, 6.0, ((0, 4),), jnp.float32)
    subset_points = draw_subset_points(jax.random.fold_in(splits[7], 71), 0)
    eigvecs = scatter_about(splits[5], (SUBSET, Q), SUBSET ** -0.5, 0.125, ((0, 64),), jnp.float32)
    shrink = jnp.clip(jnp.exp(jax.random.uniform(splits[6], (Q,), jnp.float32, math.log(0.05), math.log(0.95))), 0.05, 0.95)
    return {"centers": centers, "weights": weights, "batch_index": batch_index, "targets": targets, "subset_points": subset_points, "eigvecs": eigvecs, "shrink": shrink}


HIGH = lax.Precision.HIGHEST

def kernel(left, right):
    cross = jnp.dot(left, right.T, preferred_element_type=jnp.float32)
    left_sq = lax.optimization_barrier(jnp.sum(jnp.square(left.astype(jnp.float32)), axis=1))
    right_sq = lax.optimization_barrier(jnp.sum(jnp.square(right.astype(jnp.float32)), axis=1))
    dist_sq = left_sq[:, None] + right_sq[None, :] - 2.0 * cross
    return jnp.exp(-jnp.sqrt(jnp.maximum(dist_sq, 0.0)))

def reference(centers, weights, batch_index, targets, subset_points, eigvecs, shrink):
    batch = centers[batch_index]
    blocks = centers.reshape(N_CENTER, P_DEV, D)
    wblocks = weights.reshape(N_CENTER, P_DEV, OUTS)

    def add_block(total, pair):
        zblock, wblock = pair
        return (total + jnp.dot(kernel(batch, zblock), wblock, precision=HIGH), None)
    pred, unused = lax.scan(add_block, jnp.zeros((BATCH, OUTS), jnp.float32), (blocks, wblocks))
    resid = pred - targets
    subset_kernel = kernel(subset_points, batch)
    proj = jnp.dot(eigvecs.T, jnp.dot(subset_kernel, resid, precision=HIGH), precision=HIGH)
    lift = jnp.dot(eigvecs, shrink[:, None] * proj, precision=HIGH)

    def block_step(zblock):
        grad = jnp.dot(kernel(zblock, batch), resid, precision=HIGH)
        corr = jnp.dot(kernel(zblock, subset_points), lift, precision=HIGH)
        return (grad - corr) / jnp.sqrt(jnp.float32(BATCH))
    return lax.map(block_step, blocks).reshape(CENTERS, OUTS)
```

```python
import jax
import jax.numpy as jnp
from jax import lax
from jax.experimental import pallas as pl
from jax.experimental.pallas import tpu as pltpu
from jax.sharding import PartitionSpec as P

MESH = pl.DeviceIdType.MESH
NY, NXH, NZ = 4, 2, 8
NX = 4
NYZ = NY * NZ
D, HALF, OUTS, Q, QP = 768, 384, 256, 200, 256
ROWS, BD, BATCH, SUBSET = 2048, 256, 1024, 2048
BF, F32 = jnp.bfloat16, jnp.float32
NT = (((1,), (1,)), ((), ()))
NN = (((1,), (0,)), ((), ()))


def dot(a, b, dims=NN):
    return lax.dot_general(a, b, dims, preferred_element_type=F32)


def split(x):
    hi = x.astype(BF)
    return hi, (x - hi.astype(F32)).astype(BF)


def dot3(ah, al, bh, bl, dims=NN):
    return dot(ah, bh, dims) + dot(ah, bl, dims) + dot(al, bh, dims)


def laplace(left_sq, right_sq, cross):
    dist_sq = jnp.maximum(left_sq + right_sq - 2.0 * cross, 1e-30)
    return jnp.exp(-(dist_sq * lax.rsqrt(dist_sq)))


def col_sq(x):
    sq = jnp.sum(jnp.square(x.astype(F32)), axis=1, keepdims=True)
    return jnp.broadcast_to(sq, (x.shape[0], 128))


def row_sq(x):
    hi, lo = split(jnp.square(x.astype(F32)))
    ones = jnp.ones((8, x.shape[1]), BF)
    return dot(ones, hi, NT) + dot(ones, lo, NT)


def widen(col, n):
    return jnp.concatenate([col] * (n // 128), axis=1)


def body(
    idx_ref, shr_ref, c_hbm, w_hbm, t_hbm, s_hbm, e_hbm, out_hbm,
    c_v, w_v, t_v, e_v, e_pad, out_v,
    chosen, rsb, xsb, xrb, ball, sbuf, ebuf,
    wt, tt, c_col, b_col, b_row, s_row, kcb,
    pred, rsp, xsp, xrp, rall, rhl, gbuf, mbuf, hbuf,
    lsem, osem, ss_yz, rs_yz, ss_m, rs_m,
):
    dp, ce = lax.axis_index("dp"), lax.axis_index("center")
    xlo, core = lax.div(dp, 2), lax.rem(dp, 2)
    y, xhi, z = lax.div(ce, 16), lax.rem(lax.div(ce, 8), 2), lax.rem(ce, 8)
    x = xhi * 2 + xlo
    chunk = y * NZ + z
    first = ce * ROWS

    def yz_peer(k):
        py = lax.rem(y + lax.div(k, NZ), NY)
        pz = lax.rem(z + lax.rem(k, NZ), NZ)
        return (dp, (py * NXH + xhi) * NZ + pz), py * NZ + pz

    def z_peer(j):
        return (dp, (y * NXH + xhi) * NZ + lax.rem(z + j, NZ))

    def y_peer(j):
        return (dp, (lax.rem(y + j, NY) * NXH + xhi) * NZ + z)

    def x_peer(j):
        px = lax.rem(x + j, NX)
        return (lax.rem(px, 2) * 2 + core, (y * NXH + lax.div(px, 2)) * NZ + z)

    sib = (xlo * 2 + 1 - core, ce)
    dpx = (1 - xlo) * 2 + core

    used = []

    def remote(src, dst, peer):
        slot = len(used)
        used.append(None)
        cp = pltpu.make_async_remote_copy(
            src_ref=src, dst_ref=dst, send_sem=ss_m.at[slot], recv_sem=rs_m.at[slot],
            device_id=peer, device_id_type=MESH,
        )
        cp.start()
        used[slot] = cp
        return cp

    def yz_copy(phase, k, src, dst, peer):
        return pltpu.make_async_remote_copy(
            src_ref=src, dst_ref=dst, send_sem=ss_yz.at[phase, k - 1],
            recv_sem=rs_yz.at[phase, k - 1], device_id=peer, device_id_type=MESH,
        )

    def recv(copies):
        for cp in copies:
            cp.wait_recv()

    def local(i, src, dst):
        cp = pltpu.make_async_copy(src, dst, lsem.at[i])
        cp.start()
        return cp

    ld_c = local(0, c_hbm, c_v)
    ld_e = local(1, e_hbm, e_v)
    ld_s = local(
        2,
        s_hbm.at[pl.ds(pl.multiple_of(xlo * 16, 16), 16), pl.ds(pl.multiple_of(core * HALF, 128), HALF)],
        sbuf.at[core, y, x, z],
    )
    ld_t = local(3, t_hbm, t_v)
    ld_w = local(4, w_hbm, w_v)

    barrier = pltpu.get_barrier_semaphore()

    def greet(k, carry):
        pl.semaphore_signal(barrier, inc=1, device_id=yz_peer(k)[0], device_id_type=MESH)
        return carry

    lax.fori_loop(1, NYZ, greet, 0)
    for j in range(1, NX):
        pl.semaphore_signal(barrier, inc=1, device_id=x_peer(j), device_id_type=MESH)
    pl.semaphore_signal(barrier, inc=1, device_id=sib, device_id_type=MESH)

    e_pad[...] = jnp.zeros_like(e_pad)
    ld_e.wait()
    e_pad[:, :Q] = e_v[...]
    e_hi, e_lo = split(e_pad[pl.ds(pl.multiple_of(xlo * 16, 16), 16), :])
    ebuf[core, x, y, z] = jnp.where(core == 0, e_hi.astype(F32), e_lo.astype(F32)).astype(BF)
    idx_col = jnp.transpose(jnp.broadcast_to((idx_ref[...] - first).astype(F32), (128, BD)))
    ld_c.wait()
    chosen_f = jnp.zeros((BD, D), F32)
    for b in range(ROWS // 256):
        iota = lax.broadcasted_iota(jnp.int32, (BD, 256), 1).astype(F32) + float(b * 256)
        pick = jnp.where(widen(idx_col, 256) == iota, 1.0, 0.0).astype(BF)
        chosen_f += dot(pick, c_v[b * 256:(b + 1) * 256, :])
    chosen_b = chosen_f.astype(BF)
    chosen[0:16] = chosen_b[:, :HALF].reshape(16, 16, HALF)
    chosen[16:32] = chosen_b[:, HALF:].reshape(16, 16, HALF)
    ld_s.wait()
    pl.semaphore_wait(barrier, NYZ - 1 + NX)

    def send_b(k, carry):
        peer, pc = yz_peer(k)
        yz_copy(0, k, chosen.at[pc], rsb.at[k - 1], peer).start()
        return carry

    lax.fori_loop(1, NYZ, send_b, 0)

    s_z = [remote(sbuf.at[core, y, x, z], sbuf.at[core, y, x, z], z_peer(j)) for j in range(1, NZ)]
    e_z = [remote(ebuf.at[core, x, y, z], ebuf.at[core, x, y, z], z_peer(j)) for j in range(1, NZ)]

    ld_w.wait()

    def prep(b, carry):
        rows = pl.ds(pl.multiple_of(b * 256, 256), 256)
        hi, lo = split(jnp.transpose(w_v[rows, :]))
        wt[0, b] = hi
        wt[1, b] = lo
        c_col[rows, :] = col_sq(c_v[rows, :])
        return carry

    lax.fori_loop(0, ROWS // 256, prep, 0)
    ld_t.wait()
    tt[...] = jnp.transpose(t_v[...]).reshape(NYZ, 8, BD)

    def add_b(k, acc):
        yz_copy(0, k, chosen.at[0], rsb.at[k - 1], sib).wait_recv()
        return acc + rsb[k - 1].astype(F32)

    part_b = lax.fori_loop(1, NYZ, add_b, chosen[chunk].astype(F32))
    xsb[...] = part_b.astype(BF)
    b_x = remote(xsb, xrb, x_peer(2))
    recv(s_z)
    s_x = [remote(sbuf.at[core, y, x], sbuf.at[core, y, x], x_peer(j)) for j in range(1, NX)]
    recv(e_z)
    e_y = [remote(ebuf.at[core, x, y], ebuf.at[core, x, y], y_peer(j)) for j in range(1, NY)]
    recv([b_x])
    ball[dp, chunk] = (part_b + xrb[...].astype(F32)).astype(BF)

    def send_b2(k, carry):
        peer, pc = yz_peer(k)
        yz_copy(1, k, ball.at[dp, chunk], ball.at[dp, chunk], peer).start()
        return carry

    lax.fori_loop(1, NYZ, send_b2, 0)
    recv(s_x)
    s_y = [remote(sbuf.at[core, y], sbuf.at[core, y], y_peer(j)) for j in range(1, NY)]
    recv(e_y)
    e_x = [remote(ebuf.at[core, x], ebuf.at[core, x], x_peer(j)) for j in range(1, NX)]

    def got_b2(k, carry):
        yz_copy(1, k, ball.at[dp, chunk], ball.at[dp, chunk], sib).wait_recv()
        return carry

    lax.fori_loop(1, NYZ, got_b2, 0)
    b_r = remote(ball.at[dp, pl.ds(0, 16)], ball.at[dp, pl.ds(0, 16)], x_peer(1))
    b_l = remote(ball.at[dp, pl.ds(16, 16)], ball.at[dp, pl.ds(16, 16)], x_peer(3))
    b_s = [remote(ball.at[dp], ball.at[dp], sib)]

    def b_halves(d):
        return ball[d, 0:16].reshape(BD, HALF), ball[d, 16:32].reshape(BD, HALF)

    def norms_b(d):
        b0, b1 = b_halves(d)
        b_row[d] = row_sq(b0) + row_sq(b1)
        b_col[d] = col_sq(b0) + col_sq(b1)

    def k_rows(d, b, b0, b1):
        rows = pl.ds(pl.multiple_of(b * 256, 256), 256)
        cross = dot(c_v[rows, :HALF], b0, NT) + dot(c_v[rows, HALF:], b1, NT)
        kern = laplace(widen(c_col[rows, :], BD), b_row[d][0:1, :], cross)
        kcb[d, rows, :] = kern
        return kern

    def k_block(d):
        norms_b(d)
        b0, b1 = b_halves(d)

        def step(b, carry):
            k_rows(d, b, b0, b1)
            return carry

        lax.fori_loop(0, ROWS // 256, step, 0)

    norms_b(dp)
    own0, own1 = b_halves(dp)

    pred[...] = jnp.zeros_like(pred)

    def pred_step(b, carry):
        kh, kl = split(k_rows(dp, b, own0, own1))
        pred[...] += dot3(wt[0, b], wt[1, b], kh, kl).reshape(NYZ, 8, BD)
        return carry

    lax.fori_loop(0, ROWS // 256, pred_step, 0)

    def send_p(k, carry):
        peer, pc = yz_peer(k)
        yz_copy(2, k, pred.at[pc], rsp.at[k - 1], peer).start()
        return carry

    lax.fori_loop(1, NYZ, send_p, 0)
    recv([b_r, b_l])
    b_s += [remote(ball.at[dpx], ball.at[dpx], sib)]
    k_block(dpx)

    def add_p(k, acc):
        yz_copy(2, k, pred.at[0], rsp.at[k - 1], sib).wait_recv()
        return acc + rsp[k - 1]

    part_p = lax.fori_loop(1, NYZ, add_p, pred[chunk])
    xsp[...] = part_p
    p_x = remote(xsp, xrp, x_peer(2))
    recv(e_x)
    e_s = [remote(ebuf.at[core], ebuf.at[core], sib)]
    recv([p_x])
    rall[dp, chunk] = part_p + xrp[...] - tt[chunk]
    r_z = [remote(rall.at[dp, chunk], rall.at[dp, chunk], z_peer(j)) for j in range(1, NZ)]
    recv(b_s)
    k_block(xlo * 2 + 1 - core)
    line = pl.ds(pl.multiple_of(y * NZ, NZ), NZ)
    recv(r_z)
    r_y = [remote(rall.at[dp, line], rall.at[dp, line], y_peer(j)) for j in range(1, NY)]
    recv(s_y)
    s_s = [remote(sbuf.at[core], sbuf.at[core], sib)]
    k_block((1 - xlo) * 2 + 1 - core)
    recv(r_y)
    r_r = remote(rall.at[dp, pl.ds(0, 16)], rall.at[dp, pl.ds(0, 16)], x_peer(1))
    r_l = remote(rall.at[dp, pl.ds(16, 16)], rall.at[dp, pl.ds(16, 16)], x_peer(3))
    r_s = [remote(rall.at[dp], rall.at[dp], sib)]
    recv(e_s + s_s)

    for yy in range(NY):
        s_row[yy] = row_sq(sbuf[0, yy].reshape(512, HALF)) + row_sq(sbuf[1, yy].reshape(512, HALF))

    def subset_product(x0, x1, left):
        acc = jnp.zeros((512, QP), F32)
        for yy in range(NY):
            cross = dot(x0, sbuf[0, yy].reshape(512, HALF), NT) + dot(x1, sbuf[1, yy].reshape(512, HALF), NT)
            kh, kl = split(laplace(widen(left, 512), s_row[yy][0:1, :], cross))
            acc += dot3(kh, kl, ebuf[0, :, yy].reshape(512, QP), ebuf[1, :, yy].reshape(512, QP))
        return acc

    def g_step(b, carry):
        rows = pl.ds(pl.multiple_of(core * 1024 + b * 512, 512), 512)
        g = subset_product(c_v[rows, :HALF], c_v[rows, HALF:], c_col[rows, :]) * shr_ref[...]
        hi, lo = split(g)
        gbuf[0, rows, :] = hi
        gbuf[1, rows, :] = lo
        return carry

    lax.fori_loop(0, 2, g_step, 0)
    g_rows = pl.ds(pl.multiple_of(core * 1024, 1024), 1024)
    gm_s = [remote(gbuf.at[:, g_rows], gbuf.at[:, g_rows], sib)]
    m_rows = pl.ds(pl.multiple_of(core * 512, 512), 512)
    two = pl.ds(core * 2, 2)
    m_hi, m_lo = split(subset_product(
        ball[two, 0:16].reshape(512, HALF), ball[two, 16:32].reshape(512, HALF), b_col[two].reshape(512, 128)
    ))
    mbuf[0, m_rows, :] = m_hi
    mbuf[1, m_rows, :] = m_lo
    gm_s += [remote(mbuf.at[:, m_rows], mbuf.at[:, m_rows], sib)]
    recv([r_r, r_l])
    r_s += [remote(rall.at[dpx], rall.at[dpx], sib)]
    recv(gm_s)

    def h_step(b, carry):
        rows = pl.ds(pl.multiple_of(b * 256, 256), 256)
        gh, gl = gbuf[0, rows, :], gbuf[1, rows, :]
        for d in range(4):
            m = slice(d * 256, (d + 1) * 256)
            hi, lo = split(kcb[d, rows, :] - dot3(gh, gl, mbuf[0, m, :], mbuf[1, m, :], NT))
            hbuf[0, d, rows, :] = hi
            hbuf[1, d, rows, :] = lo
        return carry

    lax.fori_loop(0, ROWS // 256, h_step, 0)

    recv(r_s)
    for d in range(4):
        hi, lo = split(rall[d].reshape(OUTS, BD) * (1.0 / BATCH**0.5))
        rhl[0, d] = hi
        rhl[1, d] = lo

    def out_copy(b):
        rows = pl.ds(pl.multiple_of(b * 256, 256), 256)
        return pltpu.make_async_copy(out_v.at[rows, :], out_hbm.at[rows, :], osem.at[b])

    def out_step(b, carry):
        rows = pl.ds(pl.multiple_of(b * 256, 256), 256)
        acc = jnp.zeros((256, OUTS), F32)
        for d in range(4):
            acc += dot3(hbuf[0, d, rows, :], hbuf[1, d, rows, :], rhl[0, d], rhl[1, d], NT)
        out_v[rows, :] = acc
        out_copy(b).start()
        return carry

    lax.fori_loop(0, ROWS // 256, out_step, 0)

    def out_wait(b, carry):
        out_copy(b).wait()
        return carry

    lax.fori_loop(0, ROWS // 256, out_wait, 0)

    for cp in used:
        cp.wait_send()

    def sent(k, carry):
        yz_copy(0, k, chosen.at[0], rsb.at[0], sib).wait_send()
        yz_copy(1, k, ball.at[0, 0], ball.at[0, 0], sib).wait_send()
        yz_copy(2, k, pred.at[0], rsp.at[0], sib).wait_send()
        return carry

    lax.fori_loop(1, NYZ, sent, 0)


N_MISC = 64


def shards(centers, weights, batch_index, targets, subset_points, eigvecs, shrink):
    shr = jnp.pad(shrink, (0, QP - Q)).reshape(1, QP)
    v = pltpu.VMEM
    any_spec = pl.BlockSpec(memory_space=pl.ANY)
    vm = pl.BlockSpec(memory_space=pltpu.VMEM)
    return pl.pallas_call(
        body,
        out_shape=jax.ShapeDtypeStruct((ROWS, OUTS), F32),
        in_specs=[vm, vm] + [any_spec] * 5,
        out_specs=any_spec,
        scratch_shapes=[
            v((ROWS, D), BF), v((ROWS, OUTS), F32), v((BD, OUTS), F32), v((32, Q), F32), v((32, QP), F32), v((ROWS, OUTS), F32),
            v((NYZ, 16, HALF), BF), v((NYZ - 1, 16, HALF), BF), v((16, HALF), BF), v((16, HALF), BF), v((4, NYZ, 16, HALF), BF),
            v((2, NY, NX, NZ, 16, HALF), BF), v((2, NX, NY, NZ, 16, QP), BF),
            v((2, ROWS // 256, OUTS, 256), BF), v((NYZ, 8, BD), F32), v((ROWS, 128), F32), v((4, BD, 128), F32), v((4, 8, BD), F32), v((NY, 8, 512), F32), v((4, ROWS, BD), F32),
            v((NYZ, 8, BD), F32), v((NYZ - 1, 8, BD), F32), v((8, BD), F32), v((8, BD), F32), v((4, NYZ, 8, BD), F32), v((2, 4, OUTS, BD), BF),
            v((2, ROWS, QP), BF), v((2, BATCH, QP), BF), v((2, 4, ROWS, BD), BF),
            pltpu.SemaphoreType.DMA((5,)), pltpu.SemaphoreType.DMA((ROWS // 256,)),
            pltpu.SemaphoreType.DMA((3, NYZ - 1)), pltpu.SemaphoreType.DMA((3, NYZ - 1)),
            pltpu.SemaphoreType.DMA((N_MISC,)), pltpu.SemaphoreType.DMA((N_MISC,)),
        ],
        compiler_params=pltpu.CompilerParams(collective_id=0, has_side_effects=True, vmem_limit_bytes=60 * 2**20),
        name="eigenpro_step",
    )(batch_index.reshape(1, BD), shr, centers, weights, targets, subset_points, eigvecs)


def solution(mesh):
    return jax.shard_map(
        shards,
        mesh=mesh,
        in_specs=(
            P("center", None),
            P("center", None),
            P("dp"),
            P("dp", None),
            P("center", None),
            P("center", None),
            P(),
        ),
        out_specs=P("center", None),
        check_vma=False,
    )
```

```python
import jax
import jax.numpy as jnp
from jax import lax
from jax.experimental import pallas as pl
from jax.experimental.pallas import tpu as pltpu
from jax.sharding import PartitionSpec as P

MESH = pl.DeviceIdType.MESH
NY, NXH, NZ = 4, 2, 8
NX = 4
NYZ = NY * NZ
D, HALF, OUTS, Q, QP = 768, 384, 256, 200, 256
ROWS, BD, BATCH, SUBSET = 2048, 256, 1024, 2048
BF, F32 = jnp.bfloat16, jnp.float32
FAR_Z = (4, 3, 5, 2, 6, 1, 7)
NT = (((1,), (1,)), ((), ()))
NN = (((1,), (0,)), ((), ()))


def dot(a, b, dims=NN):
    return lax.dot_general(a, b, dims, preferred_element_type=F32)


def split(x):
    hi = x.astype(BF)
    return hi, (x - hi.astype(F32)).astype(BF)


def dot3(ah, al, bh, bl, dims=NN):
    return dot(ah, bh, dims) + dot(ah, bl, dims) + dot(al, bh, dims)


def laplace(left_sq, right_sq, cross):
    dist_sq = jnp.maximum(left_sq + right_sq - 2.0 * cross, 1e-30)
    return jnp.exp(-(dist_sq * lax.rsqrt(dist_sq)))


def col_sq(x):
    sq = jnp.sum(jnp.square(x.astype(F32)), axis=1, keepdims=True)
    return jnp.broadcast_to(sq, (x.shape[0], 128))


def row_sq(x):
    hi, lo = split(jnp.square(x.astype(F32)))
    ones = jnp.ones((8, x.shape[1]), BF)
    return dot(ones, hi, NT) + dot(ones, lo, NT)


def widen(col, n):
    return jnp.concatenate([col] * (n // 128), axis=1)


def body(
    idx_ref, shr_ref, c_hbm, w_hbm, t_hbm, s_hbm, e_hbm, out_ref,
    c_v, w_v, t_v, e_v, e_pad, shr_pad,
    chosen, rsby, zsrc, rsbz, xsb, xrb, ball, sbuf, ebuf,
    wt, tt, c_col, b_row, s_row, kb,
    pred, rsp, xsp, xrp, rall, rhl, gbuf, mbuf, lacc,
    lsem, ss_yz, rs_yz, ss_m, rs_m,
):
    dp, ce = lax.axis_index("dp"), lax.axis_index("center")
    xlo, core = lax.div(dp, 2), lax.rem(dp, 2)
    y, xhi, z = lax.div(ce, 16), lax.rem(lax.div(ce, 8), 2), lax.rem(ce, 8)
    x = xhi * 2 + xlo
    chunk = y * NZ + z
    first = ce * ROWS

    def yz_peer(k):
        py = lax.rem(y + lax.div(k, NZ), NY)
        pz = lax.rem(z + lax.rem(k, NZ), NZ)
        return (dp, (py * NXH + xhi) * NZ + pz), py * NZ + pz

    def z_peer(j):
        return (dp, (y * NXH + xhi) * NZ + lax.rem(z + j, NZ))

    def y_peer(j):
        return (dp, (lax.rem(y + j, NY) * NXH + xhi) * NZ + z)

    def x_peer(j):
        px = lax.rem(x + j, NX)
        return (lax.rem(px, 2) * 2 + core, (y * NXH + lax.div(px, 2)) * NZ + z)

    sib = (xlo * 2 + 1 - core, ce)
    dpx = (1 - xlo) * 2 + core
    dps, dpxs = xlo * 2 + 1 - core, (1 - xlo) * 2 + 1 - core

    def slot(py, pz):
        return lax.rem(py, 2) * NZ + pz, slice(None), pl.ds(pl.multiple_of(lax.div(py, 2) * HALF, 128), HALF)

    lane = pl.ds(pl.multiple_of(core * HALF, 128), HALF)
    used, unsent = [], []

    def remote(src, dst, peer):
        slot = len(used)
        used.append(None)
        cp = pltpu.make_async_remote_copy(
            src_ref=src, dst_ref=dst, send_sem=ss_m.at[slot], recv_sem=rs_m.at[slot],
            device_id=peer, device_id_type=MESH,
        )
        cp.start()
        unsent.append(cp)
        return cp

    def drain():
        for cp in unsent:
            cp.wait_send()
        unsent.clear()

    def yz_copy(phase, k, src, dst, peer):
        return pltpu.make_async_remote_copy(
            src_ref=src, dst_ref=dst, send_sem=ss_yz.at[phase, k - 1],
            recv_sem=rs_yz.at[phase, k - 1], device_id=peer, device_id_type=MESH,
        )

    def recv(copies):
        for cp in copies:
            cp.wait_recv()

    def local(i, src, dst):
        cp = pltpu.make_async_copy(src, dst, lsem.at[i])
        cp.start()
        return cp

    ld_c = local(0, c_hbm, c_v)
    ld_e = local(1, e_hbm, e_v)
    ld_s = local(
        2,
        s_hbm.at[pl.ds(pl.multiple_of(xlo * 16, 16), 16), lane],
        sbuf.at[x, y, z, :, lane],
    )
    ld_t = local(3, t_hbm, t_v)
    ld_w = local(4, w_hbm, w_v)

    barrier = pltpu.get_barrier_semaphore()

    def greet(k, carry):
        pl.semaphore_signal(barrier, inc=1, device_id=yz_peer(k)[0], device_id_type=MESH)
        return carry

    lax.fori_loop(1, NYZ, greet, 0)
    for j in range(1, NX):
        pl.semaphore_signal(barrier, inc=1, device_id=x_peer(j), device_id_type=MESH)
    pl.semaphore_signal(barrier, inc=1, device_id=sib, device_id_type=MESH)

    e_pad[...] = jnp.zeros_like(e_pad)
    ld_e.wait()
    e_pad[:, :Q] = e_v[...]
    shr_pad[...] = jnp.zeros_like(shr_pad)
    shr_pad[0:1, :Q] = shr_ref[...]
    e_hi, e_lo = split(e_pad[pl.ds(pl.multiple_of(xlo * 16, 16), 16), :])
    ebuf[core, y, x, z] = jnp.where(core == 0, e_hi.astype(F32), e_lo.astype(F32)).astype(BF)
    idx_col = jnp.transpose(jnp.broadcast_to((idx_ref[...] - first).astype(F32), (128, BD)))
    ld_c.wait()
    chosen_f = jnp.zeros((BD, D), F32)
    for b in range(ROWS // 256):
        iota = lax.broadcasted_iota(jnp.int32, (BD, 256), 1).astype(F32) + float(b * 256)
        pick = jnp.where(widen(idx_col, 256) == iota, 1.0, 0.0).astype(BF)
        chosen_f += dot(pick, c_v[b * 256:(b + 1) * 256, :])
    chosen_b = chosen_f.astype(BF)
    chosen[...] = chosen_b.reshape(16, 16, D)
    ld_s.wait()
    pl.semaphore_wait(barrier, NYZ - 1 + NX)

    b_y = []
    for i, o in enumerate(FAR_Z + (0,)):
        pz = lax.rem(z + o, NZ)
        b_y.append([
            remote(chosen.at[slot(lax.rem(y + j, NY), pz)], rsby.at[i, j - 1], y_peer(j)) for j in range(1, NY)
        ])

    s_z = [remote(sbuf.at[x, y, z, :, lane], sbuf.at[x, y, z, :, lane], z_peer(o)) for o in FAR_Z]
    e_z = [remote(ebuf.at[core, y, x, z], ebuf.at[core, y, x, z], z_peer(o)) for o in FAR_Z]

    b_z = []
    for i, o in enumerate(FAR_Z + (0,)):
        recv(b_y[i])
        part_b = chosen[slot(y, lax.rem(z + o, NZ))].astype(F32)
        for j in range(NY - 1):
            part_b += rsby[i, j].astype(F32)
        if o:
            zsrc[i] = part_b.astype(BF)
            b_z.append(remote(zsrc.at[i], rsbz.at[i], z_peer(o)))
    recv(s_z)
    s_y = [remote(sbuf.at[x, y, :, :, lane], sbuf.at[x, y, :, :, lane], y_peer(j)) for j in range(1, NY)]
    recv(e_z)
    e_x = [remote(ebuf.at[core, y, x], ebuf.at[core, y, x], x_peer(j)) for j in range(1, NX)]
    for i in range(NZ - 1):
        recv([b_z[i]])
        part_b += rsbz[i].astype(F32)
    xsb[...] = part_b.astype(BF)
    b_x = remote(xsb, xrb, x_peer(2))
    ld_w.wait()

    def prep(b, carry):
        rows = pl.ds(pl.multiple_of(b * 256, 256), 256)
        hi, lo = split(jnp.transpose(w_v[rows, :]))
        wt[0, b] = hi
        wt[1, b] = lo
        c_col[rows, :] = col_sq(c_v[rows, :])
        return carry

    lax.fori_loop(0, ROWS // 256, prep, 0)
    ld_t.wait()
    tt[...] = jnp.transpose(t_v[...]).reshape(NYZ, 8, BD)

    recv([b_x])
    here = (dp,) + slot(y, z)
    ball[here] = (xsb[...].astype(F32) + xrb[...].astype(F32)).astype(BF)

    own = ball.at[here]
    g_z = {o: remote(own, own, z_peer(o)) for o in FAR_Z}
    g_y = [remote(own, own, y_peer(j)) for j in range(1, NY)]
    recv(s_y)
    s_x = [remote(sbuf.at[x, :, :, :, lane], sbuf.at[x, :, :, :, lane], x_peer(j)) for j in range(1, NX)]
    s_s = [remote(sbuf.at[x, :, :, :, lane], sbuf.at[x, :, :, :, lane], sib)]
    for o in FAR_Z[::-1]:
        recv([g_z[o]])
        came = ball.at[(dp,) + slot(y, lax.rem(z + NZ - o, NZ))]
        g_y += [remote(came, came, y_peer(j)) for j in range(1, NY)]
    recv(e_x)
    e_y = [remote(ebuf.at[core, y], ebuf.at[core, y], y_peer(j)) for j in range(1, NY)]
    e_s = [remote(ebuf.at[core, y], ebuf.at[core, y], sib)]
    recv(g_y)
    b_s = [remote(ball.at[dp], ball.at[dp], sib)]
    b_r = remote(ball.at[dp, pl.ds(0, 8)], ball.at[dp, pl.ds(0, 8)], x_peer(1))
    b_l = remote(ball.at[dp, pl.ds(8, 8)], ball.at[dp, pl.ds(8, 8)], x_peer(3))

    def norms_b(d):
        b_row[d] = row_sq(ball[d].reshape(BD, D))

    def k_rows(d, b, n):
        rows = pl.ds(pl.multiple_of(b * n, n), n)
        cross = dot(c_v[rows, :], ball[d].reshape(BD, D), NT)
        hi, lo = split(laplace(widen(c_col[rows, :], BD), b_row[d][0:1, :], cross))
        kb[0, d, rows, :] = hi
        kb[1, d, rows, :] = lo
        return hi, lo

    def k_block(d):
        norms_b(d)

        def step(b, carry):
            k_rows(d, b, 512)
            return carry

        lax.fori_loop(0, ROWS // 512, step, 0, unroll=True)

    norms_b(dp)
    pred[...] = jnp.zeros_like(pred)

    def pred_step(b, carry):
        kh, kl = k_rows(dp, b, 256)
        pred[...] += dot3(wt[0, b], wt[1, b], kh, kl).reshape(NYZ, 8, BD)
        return carry

    lax.fori_loop(0, ROWS // 256, pred_step, 0, unroll=True)

    def send_p(i, carry):
        k = NYZ - i
        peer, pc = yz_peer(k)
        yz_copy(0, k, pred.at[pc], rsp.at[k - 1], peer).start()
        return carry

    lax.fori_loop(1, NYZ, send_p, 0)
    recv(b_s)
    k_block(dps)
    drain()
    recv([b_r, b_l])
    b_s2 = remote(ball.at[dpx], ball.at[dpx], sib)
    k_block(dpx)
    recv(e_y)
    e_s += [remote(ebuf.at[core, lax.rem(y + j, NY)], ebuf.at[core, lax.rem(y + j, NY)], sib) for j in range(1, NY)]
    recv([b_s2])
    k_block(dpxs)

    def subset_product(rows_b, left):
        n = rows_b.shape[0]
        acc = jnp.zeros((n, QP), F32)
        for xx in range(NX):
            for p in range(NY // 2):
                two = slice(2 * p, 2 * p + 2)
                cross = dot(rows_b, sbuf[xx, two].reshape(256, D), NT)
                kh, kl = split(laplace(widen(left, 256), s_row[xx][0:1, 256 * p:256 * p + 256], cross))
                acc += dot3(kh, kl, ebuf[0, two, xx].reshape(256, QP), ebuf[1, two, xx].reshape(256, QP))
        return acc

    def g_step(b):
        rows = pl.ds(pl.multiple_of(core * 1024 + b * 512, 512), 512)
        g = subset_product(c_v[rows, :], c_col[rows, :]) * -shr_pad[0:1, :]
        hi, lo = split(g)
        gbuf[0, rows, :] = hi
        gbuf[1, rows, :] = lo

    def add_p(k, acc):
        yz_copy(0, k, pred.at[0], rsp.at[k - 1], sib).wait_recv()
        return acc + rsp[k - 1]

    part_p = lax.fori_loop(1, NYZ, add_p, pred[chunk])
    xsp[...] = part_p
    p_x = remote(xsp, xrp, x_peer(2))
    recv([p_x])
    rall[dp, chunk] = xsp[...] + xrp[...] - tt[chunk]

    def send_r(i, carry):
        k = NYZ - i
        peer, pc = yz_peer(k)
        yz_copy(1, k, rall.at[dp, chunk], rall.at[dp, chunk], peer).start()
        return carry

    lax.fori_loop(1, NYZ, send_r, 0)
    recv(s_x)
    s_s += [remote(sbuf.at[lax.rem(x + j, NX), :, :, :, lane], sbuf.at[lax.rem(x + j, NX), :, :, :, lane], sib) for j in range(1, NX)]
    recv(e_s + s_s)
    for xx in range(NX):
        s_row[xx] = row_sq(sbuf[xx].reshape(512, D))
    b_part = ball[core * 2 + lax.div(y, 2), pl.ds(lax.rem(y, 2) * 8, 8)].reshape(128, D)
    m_mine = pl.ds(pl.multiple_of(core * 512 + y * 128, 128), 128)
    m_hi, m_lo = split(subset_product(b_part, col_sq(b_part)))
    mbuf[0, m_mine, :] = m_hi
    mbuf[1, m_mine, :] = m_lo
    m_y = [remote(mbuf.at[:, m_mine], mbuf.at[:, m_mine], y_peer(j)) for j in range(1, NY)]
    g_step(0)

    def got_r(k, carry):
        yz_copy(1, k, rall.at[dp, chunk], rall.at[dp, chunk], sib).wait_recv()
        return carry

    r_x = {}
    for j in (0, 1, 3, 2):
        lax.fori_loop(max(1, j * NZ), (j + 1) * NZ, got_r, 0)
        line_y = lax.rem(y + NY - j, NY)
        line = rall.at[dp, pl.ds(pl.multiple_of(line_y * NZ, NZ), NZ)]
        r_x[j] = remote(line, line, x_peer(1 + 2 * lax.div(line_y, 2)))
    r_s = remote(rall.at[dp], rall.at[dp], sib)
    g_step(1)
    g_rows = pl.ds(pl.multiple_of(core * 1024, 1024), 1024)
    gm_s = [remote(gbuf.at[:, g_rows], gbuf.at[:, g_rows], sib)]
    r_s2 = []
    for j in (0, 1, 3, 2):
        recv([r_x[j]])
        line = rall.at[dpx, pl.ds(pl.multiple_of(lax.rem(y + NY - j, NY) * NZ, NZ), NZ)]
        r_s2.append(remote(line, line, sib))
    recv(m_y)
    m_rows = pl.ds(pl.multiple_of(core * 512, 512), 512)
    gm_s += [remote(mbuf.at[:, m_rows], mbuf.at[:, m_rows], sib)]

    def split_r(d):
        hi, lo = split(rall[d].reshape(OUTS, BD) * (1.0 / BATCH**0.5))
        rhl[0, d] = hi
        rhl[1, d] = lo

    def k_out(rows, d):
        return dot3(kb[0, d, rows, :], kb[1, d, rows, :], rhl[0, d], rhl[1, d], NT)

    def lift_t(d):
        rows = pl.ds(pl.multiple_of(d * BD, BD), BD)
        return dot3(rhl[0, d], rhl[1, d], mbuf[0, rows, :], mbuf[1, rows, :])

    recv([r_s])
    split_r(dp)
    split_r(dps)

    def out_near(b, carry):
        rows = pl.ds(pl.multiple_of(b * 256, 256), 256)
        out_ref[rows, :] = k_out(rows, dp) + k_out(rows, dps)
        return carry

    lax.fori_loop(0, ROWS // 256, out_near, 0, unroll=True)
    recv(r_s2)
    split_r(dpx)
    split_r(dpxs)
    recv(gm_s)
    lacc[...] = lift_t(0) + lift_t(1) + lift_t(2) + lift_t(3)
    l_hi, l_lo = split(lacc[...])

    def out_far(b, carry):
        rows = pl.ds(pl.multiple_of(b * 256, 256), 256)
        corr = dot3(gbuf[0, rows, :], gbuf[1, rows, :], l_hi, l_lo, NT)
        out_ref[rows, :] += k_out(rows, dpx) + k_out(rows, dpxs) + corr
        return carry

    lax.fori_loop(0, ROWS // 256, out_far, 0, unroll=True)
    drain()

    def sent(k, carry):
        yz_copy(0, k, pred.at[0], rsp.at[0], sib).wait_send()
        yz_copy(1, k, rall.at[0, 0], rall.at[0, 0], sib).wait_send()
        return carry

    lax.fori_loop(1, NYZ, sent, 0)


N_MISC = 144


def shards(centers, weights, batch_index, targets, subset_points, eigvecs, shrink):
    v = pltpu.VMEM
    any_spec = pl.BlockSpec(memory_space=pl.ANY)
    vm = pl.BlockSpec(memory_space=pltpu.VMEM)
    return pl.pallas_call(
        body,
        out_shape=pltpu.VMEM((ROWS, OUTS), F32),
        in_specs=[vm, vm] + [any_spec] * 5,
        out_specs=vm,
        scratch_shapes=[
            v((ROWS, D), BF), v((ROWS, OUTS), F32), v((BD, OUTS), F32), v((32, Q), F32), v((32, QP), F32), v((8, QP), F32),
            v((16, 16, D), BF), v((NZ, NY - 1, 16, HALF), BF), v((NZ - 1, 16, HALF), BF), v((NZ - 1, 16, HALF), BF), v((16, HALF), BF), v((16, HALF), BF), v((4, 16, 16, D), BF),
            v((NX, NY, NZ, 16, D), BF), v((2, NY, NX, NZ, 16, QP), BF),
            v((2, ROWS // 256, OUTS, 256), BF), v((NYZ, 8, BD), F32), v((ROWS, 128), F32), v((4, 8, BD), F32), v((NX, 8, 512), F32), v((2, 4, ROWS, BD), BF),
            v((NYZ, 8, BD), F32), v((NYZ - 1, 8, BD), F32), v((8, BD), F32), v((8, BD), F32), v((4, NYZ, 8, BD), F32), v((2, 4, OUTS, BD), BF),
            v((2, ROWS, QP), BF), v((2, BATCH, QP), BF), v((OUTS, QP), F32),
            pltpu.SemaphoreType.DMA((5,)),
            pltpu.SemaphoreType.DMA((2, NYZ - 1)), pltpu.SemaphoreType.DMA((2, NYZ - 1)),
            pltpu.SemaphoreType.DMA((N_MISC,)), pltpu.SemaphoreType.DMA((N_MISC,)),
        ],
        compiler_params=pltpu.CompilerParams(collective_id=0, has_side_effects=True, vmem_limit_bytes=56 * 2**20),
        name="eigenpro_step",
    )(batch_index.reshape(1, BD), shrink.reshape(1, Q), centers, weights, targets, subset_points, eigvecs)


def solution(mesh):
    return jax.shard_map(
        shards,
        mesh=mesh,
        in_specs=(
            P("center", None),
            P("center", None),
            P("dp"),
            P("dp", None),
            P("center", None),
            P("center", None),
            P(),
        ),
        out_specs=P("center", None),
        check_vma=False,
    )
```

```python
import jax
import jax.numpy as jnp
from jax import lax
from jax.experimental import pallas as pl
from jax.experimental.pallas import tpu as pltpu
from jax.sharding import PartitionSpec as P

MESH = pl.DeviceIdType.MESH
NY, NXH, NZ = 4, 2, 8
NX = 4
NYZ = NY * NZ
D, HALF, OUTS, Q, QP = 768, 384, 256, 200, 256
ROWS, BD, BATCH, SUBSET = 2048, 256, 1024, 2048
BF, F32 = jnp.bfloat16, jnp.float32
FAR_Z = (4, 3, 5, 2, 6, 1, 7)
NT = (((1,), (1,)), ((), ()))
NN = (((1,), (0,)), ((), ()))


def dot(a, b, dims=NN):
    return lax.dot_general(a, b, dims, preferred_element_type=F32)


def split(x):
    hi = x.astype(BF)
    return hi, (x - hi.astype(F32)).astype(BF)


def dot3(ah, al, bh, bl, dims=NN):
    return dot(ah, bh, dims) + dot(ah, bl, dims) + dot(al, bh, dims)


def laplace(left_sq, right_sq, cross):
    dist_sq = jnp.maximum(left_sq + right_sq - 2.0 * cross, 1e-30)
    return jnp.exp(-(dist_sq * lax.rsqrt(dist_sq)))


def col_sq(x):
    sq = jnp.sum(jnp.square(x.astype(F32)), axis=1, keepdims=True)
    return jnp.broadcast_to(sq, (x.shape[0], 128))


def row_sq(x):
    hi, lo = split(jnp.square(x.astype(F32)))
    ones = jnp.ones((8, x.shape[1]), BF)
    return dot(ones, hi, NT) + dot(ones, lo, NT)


def widen(col, n):
    return jnp.concatenate([col] * (n // 128), axis=1)


def body(
    idx_ref, shr_ref, c_hbm, w_hbm, t_hbm, s_hbm, e_hbm, out_ref,
    c_v, w_v, t_v, e_v, e_pad, shr_pad,
    chosen, rsby, zsrc, rsbz, xsb, xrb, ball, sbuf, ebuf,
    wt, tt, c_col, b_row, s_row, kb,
    pred, rsp, xsp, xrp, rall, rhl, gbuf, mbuf, lacc,
    lsem, ss_yz, rs_yz, ss_m, rs_m,
):
    dp, ce = lax.axis_index("dp"), lax.axis_index("center")
    xlo, core = lax.div(dp, 2), lax.rem(dp, 2)
    y, xhi, z = lax.div(ce, 16), lax.rem(lax.div(ce, 8), 2), lax.rem(ce, 8)
    x = xhi * 2 + xlo
    chunk = y * NZ + z
    first = ce * ROWS

    def yz_peer(k):
        py = lax.rem(y + lax.div(k, NZ), NY)
        pz = lax.rem(z + lax.rem(k, NZ), NZ)
        return (dp, (py * NXH + xhi) * NZ + pz), py * NZ + pz

    def z_peer(j):
        return (dp, (y * NXH + xhi) * NZ + lax.rem(z + j, NZ))

    def y_peer(j):
        return (dp, (lax.rem(y + j, NY) * NXH + xhi) * NZ + z)

    def x_peer(j):
        px = lax.rem(x + j, NX)
        return (lax.rem(px, 2) * 2 + core, (y * NXH + lax.div(px, 2)) * NZ + z)

    sib = (xlo * 2 + 1 - core, ce)
    dpx = (1 - xlo) * 2 + core
    dps, dpxs = xlo * 2 + 1 - core, (1 - xlo) * 2 + 1 - core

    def slot(py, pz):
        return lax.rem(py, 2) * NZ + pz, slice(None), pl.ds(pl.multiple_of(lax.div(py, 2) * HALF, 128), HALF)

    lane = pl.ds(pl.multiple_of(core * HALF, 128), HALF)
    used, unsent = [], []

    def remote(src, dst, peer):
        slot = len(used)
        used.append(None)
        cp = pltpu.make_async_remote_copy(
            src_ref=src, dst_ref=dst, send_sem=ss_m.at[slot], recv_sem=rs_m.at[slot],
            device_id=peer, device_id_type=MESH,
        )
        cp.start()
        unsent.append(cp)
        return cp

    def drain():
        for cp in unsent:
            cp.wait_send()
        unsent.clear()

    def yz_copy(phase, k, src, dst, peer):
        return pltpu.make_async_remote_copy(
            src_ref=src, dst_ref=dst, send_sem=ss_yz.at[phase, k - 1],
            recv_sem=rs_yz.at[phase, k - 1], device_id=peer, device_id_type=MESH,
        )

    def recv(copies):
        for cp in copies:
            cp.wait_recv()

    def local(i, src, dst):
        cp = pltpu.make_async_copy(src, dst, lsem.at[i])
        cp.start()
        return cp

    ld_c = local(0, c_hbm, c_v)
    ld_e = local(1, e_hbm, e_v)
    ld_s = local(
        2,
        s_hbm.at[pl.ds(pl.multiple_of(xlo * 16, 16), 16), lane],
        sbuf.at[x, y, z, :, lane],
    )
    ld_t = local(3, t_hbm, t_v)
    ld_w = local(4, w_hbm, w_v)

    barrier = pltpu.get_barrier_semaphore()

    def greet(k, carry):
        pl.semaphore_signal(barrier, inc=1, device_id=yz_peer(k)[0], device_id_type=MESH)
        return carry

    lax.fori_loop(1, NYZ, greet, 0)
    for j in range(1, NX):
        pl.semaphore_signal(barrier, inc=1, device_id=x_peer(j), device_id_type=MESH)
    pl.semaphore_signal(barrier, inc=1, device_id=sib, device_id_type=MESH)

    e_pad[...] = jnp.zeros_like(e_pad)
    ld_e.wait()
    e_pad[:, :Q] = e_v[...]
    shr_pad[...] = jnp.zeros_like(shr_pad)
    shr_pad[0:1, :Q] = shr_ref[...]
    e_hi, e_lo = split(e_pad[pl.ds(pl.multiple_of(xlo * 16, 16), 16), :])
    ebuf[core, y, x, z] = jnp.where(core == 0, e_hi.astype(F32), e_lo.astype(F32)).astype(BF)
    idx_col = jnp.transpose(jnp.broadcast_to((idx_ref[...] - first).astype(F32), (128, BD)))
    ld_c.wait()
    chosen_f = jnp.zeros((BD, D), F32)
    for b in range(ROWS // 256):
        iota = lax.broadcasted_iota(jnp.int32, (BD, 256), 1).astype(F32) + float(b * 256)
        pick = jnp.where(widen(idx_col, 256) == iota, 1.0, 0.0).astype(BF)
        chosen_f += dot(pick, c_v[b * 256:(b + 1) * 256, :])
    chosen_b = chosen_f.astype(BF)
    chosen[...] = chosen_b.reshape(16, 16, D)
    ld_s.wait()
    pl.semaphore_wait(barrier, NYZ - 1 + NX)

    b_y = []
    for i, o in enumerate(FAR_Z + (0,)):
        pz = lax.rem(z + o, NZ)
        b_y.append([
            remote(chosen.at[slot(lax.rem(y + j, NY), pz)], rsby.at[i, j - 1], y_peer(j)) for j in range(1, NY)
        ])

    s_z = [remote(sbuf.at[x, y, z, :, lane], sbuf.at[x, y, z, :, lane], z_peer(o)) for o in FAR_Z]
    e_z = [remote(ebuf.at[core, y, x, z], ebuf.at[core, y, x, z], z_peer(o)) for o in FAR_Z]

    b_z = []
    for i, o in enumerate(FAR_Z + (0,)):
        recv(b_y[i])
        part_b = chosen[slot(y, lax.rem(z + o, NZ))].astype(F32)
        for j in range(NY - 1):
            part_b += rsby[i, j].astype(F32)
        if o:
            zsrc[i] = part_b.astype(BF)
            b_z.append(remote(zsrc.at[i], rsbz.at[i], z_peer(o)))
    recv(s_z)
    s_y = [remote(sbuf.at[x, y, :, :, lane], sbuf.at[x, y, :, :, lane], y_peer(j)) for j in range(1, NY)]
    recv(e_z)
    e_x = [remote(ebuf.at[core, y, x], ebuf.at[core, y, x], x_peer(j)) for j in range(1, NX)]
    for i in range(NZ - 1):
        recv([b_z[i]])
        part_b += rsbz[i].astype(F32)
    xsb[...] = part_b.astype(BF)
    b_x = remote(xsb, xrb, x_peer(2))
    ld_w.wait()

    def prep(b, carry):
        rows = pl.ds(pl.multiple_of(b * 256, 256), 256)
        hi, lo = split(jnp.transpose(w_v[rows, :]))
        wt[0, b] = hi
        wt[1, b] = lo
        c_col[rows, :] = col_sq(c_v[rows, :])
        return carry

    lax.fori_loop(0, ROWS // 256, prep, 0)
    ld_t.wait()
    tt[...] = jnp.transpose(t_v[...]).reshape(NYZ, 8, BD)

    recv([b_x])
    here = (dp,) + slot(y, z)
    ball[here] = (xsb[...].astype(F32) + xrb[...].astype(F32)).astype(BF)

    own = ball.at[here]
    g_z = {o: remote(own, own, z_peer(o)) for o in FAR_Z}
    g_y = [remote(own, own, y_peer(j)) for j in range(1, NY)]
    recv(s_y)
    s_x = [remote(sbuf.at[x, :, :, :, lane], sbuf.at[x, :, :, :, lane], x_peer(j)) for j in (1, 3)]
    s_s = [remote(sbuf.at[x, :, :, :, lane], sbuf.at[x, :, :, :, lane], sib)]
    for o in FAR_Z[::-1]:
        recv([g_z[o]])
        came = ball.at[(dp,) + slot(y, lax.rem(z + NZ - o, NZ))]
        g_y += [remote(came, came, y_peer(j)) for j in range(1, NY)]
    recv(e_x)
    e_y = [remote(ebuf.at[core, y], ebuf.at[core, y], y_peer(j)) for j in range(1, NY)]
    e_s = [remote(ebuf.at[core, y], ebuf.at[core, y], sib)]
    recv(g_y)
    b_s = [remote(ball.at[dp], ball.at[dp], sib)]
    b_r = remote(ball.at[dp, pl.ds(0, 8)], ball.at[dp, pl.ds(0, 8)], x_peer(1))
    b_l = remote(ball.at[dp, pl.ds(8, 8)], ball.at[dp, pl.ds(8, 8)], x_peer(3))

    def norms_b(d):
        b_row[d] = row_sq(ball[d].reshape(BD, D))

    def k_rows(d, b, n):
        rows = pl.ds(pl.multiple_of(b * n, n), n)
        cross = dot(c_v[rows, :], ball[d].reshape(BD, D), NT)
        hi, lo = split(laplace(widen(c_col[rows, :], BD), b_row[d][0:1, :], cross))
        kb[0, d, rows, :] = hi
        kb[1, d, rows, :] = lo
        return hi, lo

    def k_block(d):
        norms_b(d)

        def step(b, carry):
            k_rows(d, b, 512)
            return carry

        lax.fori_loop(0, ROWS // 512, step, 0, unroll=True)

    norms_b(dp)
    pred[...] = jnp.zeros_like(pred)

    def pred_step(b, carry):
        kh, kl = k_rows(dp, b, 256)
        pred[...] += dot3(wt[0, b], wt[1, b], kh, kl).reshape(NYZ, 8, BD)
        return carry

    lax.fori_loop(0, ROWS // 256, pred_step, 0, unroll=True)

    def send_p(i, carry):
        k = NYZ - i
        peer, pc = yz_peer(k)
        yz_copy(0, k, pred.at[pc], rsp.at[k - 1], peer).start()
        return carry

    lax.fori_loop(1, NYZ, send_p, 0)
    recv(b_s)
    k_block(dps)
    recv(s_x)
    west = sbuf.at[lax.rem(x + 3, NX), :, :, :, lane]
    east = sbuf.at[lax.rem(x + 1, NX), :, :, :, lane]
    west_half = sbuf.at[lax.rem(x + 3, NX), pl.ds(0, 2), :, :, lane]
    east_half = sbuf.at[lax.rem(x + 1, NX), pl.ds(2, 2), :, :, lane]
    s_f = [remote(west_half, west_half, x_peer(1)), remote(east_half, east_half, x_peer(3))]
    s_s += [remote(west, west, sib), remote(east, east, sib)]
    recv([b_r, b_l])
    b_s2 = remote(ball.at[dpx], ball.at[dpx], sib)
    k_block(dpx)
    recv(e_y)
    e_s += [remote(ebuf.at[core, lax.rem(y + j, NY)], ebuf.at[core, lax.rem(y + j, NY)], sib) for j in range(1, NY)]
    recv([b_s2])
    k_block(dpxs)

    def subset_product(rows_b, left):
        n = rows_b.shape[0]
        acc = jnp.zeros((n, QP), F32)
        for xx in range(NX):
            for p in range(NY // 2):
                two = slice(2 * p, 2 * p + 2)
                cross = dot(rows_b, sbuf[xx, two].reshape(256, D), NT)
                kh, kl = split(laplace(widen(left, 256), s_row[xx][0:1, 256 * p:256 * p + 256], cross))
                acc += dot3(kh, kl, ebuf[0, two, xx].reshape(256, QP), ebuf[1, two, xx].reshape(256, QP))
        return acc

    def g_step(b):
        rows = pl.ds(pl.multiple_of(core * 1024 + b * 512, 512), 512)
        g = subset_product(c_v[rows, :], c_col[rows, :]) * -shr_pad[0:1, :]
        hi, lo = split(g)
        gbuf[0, rows, :] = hi
        gbuf[1, rows, :] = lo

    def add_p(k, acc):
        yz_copy(0, k, pred.at[0], rsp.at[k - 1], sib).wait_recv()
        return acc + rsp[k - 1]

    part_p = lax.fori_loop(1, NYZ, add_p, pred[chunk])
    xsp[...] = part_p
    p_x = remote(xsp, xrp, x_peer(2))
    recv(s_f)
    s_s += [remote(sbuf.at[lax.rem(x + 2, NX), :, :, :, lane], sbuf.at[lax.rem(x + 2, NX), :, :, :, lane], sib)]
    recv([p_x])
    rall[dp, chunk] = xsp[...] + xrp[...] - tt[chunk]

    def send_r(i, carry):
        k = NYZ - i
        peer, pc = yz_peer(k)
        yz_copy(1, k, rall.at[dp, chunk], rall.at[dp, chunk], peer).start()
        return carry

    lax.fori_loop(1, NYZ, send_r, 0)
    recv(e_s + s_s)
    for xx in range(NX):
        s_row[xx] = row_sq(sbuf[xx].reshape(512, D))
    b_part = ball[core * 2 + lax.div(y, 2), pl.ds(lax.rem(y, 2) * 8, 8)].reshape(128, D)
    m_mine = pl.ds(pl.multiple_of(core * 512 + y * 128, 128), 128)
    m_hi, m_lo = split(subset_product(b_part, col_sq(b_part)))
    mbuf[0, m_mine, :] = m_hi
    mbuf[1, m_mine, :] = m_lo
    m_y = [remote(mbuf.at[:, m_mine], mbuf.at[:, m_mine], y_peer(j)) for j in range(1, NY)]
    g_step(0)

    def got_r(k, carry):
        yz_copy(1, k, rall.at[dp, chunk], rall.at[dp, chunk], sib).wait_recv()
        return carry

    r_x = {}
    for j in (0, 1, 3, 2):
        lax.fori_loop(max(1, j * NZ), (j + 1) * NZ, got_r, 0)
        line_y = lax.rem(y + NY - j, NY)
        line = rall.at[dp, pl.ds(pl.multiple_of(line_y * NZ, NZ), NZ)]
        r_x[j] = remote(line, line, x_peer(1 + 2 * lax.div(line_y, 2)))
    r_s = remote(rall.at[dp], rall.at[dp], sib)
    g_step(1)
    g_rows = pl.ds(pl.multiple_of(core * 1024, 1024), 1024)
    gm_s = [remote(gbuf.at[:, g_rows], gbuf.at[:, g_rows], sib)]
    r_s2 = []
    for j in (0, 1, 3, 2):
        recv([r_x[j]])
        line = rall.at[dpx, pl.ds(pl.multiple_of(lax.rem(y + NY - j, NY) * NZ, NZ), NZ)]
        r_s2.append(remote(line, line, sib))
    recv(m_y)
    m_rows = pl.ds(pl.multiple_of(core * 512, 512), 512)
    gm_s += [remote(mbuf.at[:, m_rows], mbuf.at[:, m_rows], sib)]

    def split_r(d):
        hi, lo = split(rall[d].reshape(OUTS, BD) * (1.0 / BATCH**0.5))
        rhl[0, d] = hi
        rhl[1, d] = lo

    def k_out(rows, d):
        return dot3(kb[0, d, rows, :], kb[1, d, rows, :], rhl[0, d], rhl[1, d], NT)

    def lift_t(d):
        rows = pl.ds(pl.multiple_of(d * BD, BD), BD)
        return dot3(rhl[0, d], rhl[1, d], mbuf[0, rows, :], mbuf[1, rows, :])

    recv([r_s])
    split_r(dp)
    split_r(dps)

    def out_near(b, carry):
        rows = pl.ds(pl.multiple_of(b * 256, 256), 256)
        out_ref[rows, :] = k_out(rows, dp) + k_out(rows, dps)
        return carry

    lax.fori_loop(0, ROWS // 256, out_near, 0, unroll=True)
    recv(r_s2)
    split_r(dpx)
    split_r(dpxs)
    recv(gm_s)
    lacc[...] = lift_t(0) + lift_t(1) + lift_t(2) + lift_t(3)
    l_hi, l_lo = split(lacc[...])

    def out_far(b, carry):
        rows = pl.ds(pl.multiple_of(b * 256, 256), 256)
        corr = dot3(gbuf[0, rows, :], gbuf[1, rows, :], l_hi, l_lo, NT)
        out_ref[rows, :] += k_out(rows, dpx) + k_out(rows, dpxs) + corr
        return carry

    lax.fori_loop(0, ROWS // 256, out_far, 0, unroll=True)
    drain()

    def sent(k, carry):
        yz_copy(0, k, pred.at[0], rsp.at[0], sib).wait_send()
        yz_copy(1, k, rall.at[0, 0], rall.at[0, 0], sib).wait_send()
        return carry

    lax.fori_loop(1, NYZ, sent, 0)


N_MISC = 144


def shards(centers, weights, batch_index, targets, subset_points, eigvecs, shrink):
    v = pltpu.VMEM
    any_spec = pl.BlockSpec(memory_space=pl.ANY)
    vm = pl.BlockSpec(memory_space=pltpu.VMEM)
    return pl.pallas_call(
        body,
        out_shape=pltpu.VMEM((ROWS, OUTS), F32),
        in_specs=[vm, vm] + [any_spec] * 5,
        out_specs=vm,
        scratch_shapes=[
            v((ROWS, D), BF), v((ROWS, OUTS), F32), v((BD, OUTS), F32), v((32, Q), F32), v((32, QP), F32), v((8, QP), F32),
            v((16, 16, D), BF), v((NZ, NY - 1, 16, HALF), BF), v((NZ - 1, 16, HALF), BF), v((NZ - 1, 16, HALF), BF), v((16, HALF), BF), v((16, HALF), BF), v((4, 16, 16, D), BF),
            v((NX, NY, NZ, 16, D), BF), v((2, NY, NX, NZ, 16, QP), BF),
            v((2, ROWS // 256, OUTS, 256), BF), v((NYZ, 8, BD), F32), v((ROWS, 128), F32), v((4, 8, BD), F32), v((NX, 8, 512), F32), v((2, 4, ROWS, BD), BF),
            v((NYZ, 8, BD), F32), v((NYZ - 1, 8, BD), F32), v((8, BD), F32), v((8, BD), F32), v((4, NYZ, 8, BD), F32), v((2, 4, OUTS, BD), BF),
            v((2, ROWS, QP), BF), v((2, BATCH, QP), BF), v((OUTS, QP), F32),
            pltpu.SemaphoreType.DMA((5,)),
            pltpu.SemaphoreType.DMA((2, NYZ - 1)), pltpu.SemaphoreType.DMA((2, NYZ - 1)),
            pltpu.SemaphoreType.DMA((N_MISC,)), pltpu.SemaphoreType.DMA((N_MISC,)),
        ],
        compiler_params=pltpu.CompilerParams(collective_id=0, has_side_effects=True, vmem_limit_bytes=56 * 2**20),
        name="eigenpro_step",
    )(batch_index.reshape(1, BD), shrink.reshape(1, Q), centers, weights, targets, subset_points, eigvecs)


def solution(mesh):
    return jax.shard_map(
        shards,
        mesh=mesh,
        in_specs=(
            P("center", None),
            P("center", None),
            P("dp"),
            P("dp", None),
            P("center", None),
            P("center", None),
            P(),
        ),
        out_specs=P("center", None),
        check_vma=False,
    )
```

```python
import jax
import jax.numpy as jnp
from jax import lax
from jax.experimental import pallas as pl
from jax.experimental.pallas import tpu as pltpu
from jax.sharding import PartitionSpec as P

MESH = pl.DeviceIdType.MESH
NY, NXH, NZ = 4, 2, 8
NX = 4
NYZ = NY * NZ
D, HALF, OUTS, Q, QP = 768, 384, 256, 200, 256
ROWS, BD, BATCH, SUBSET = 2048, 256, 1024, 2048
BF, F32 = jnp.bfloat16, jnp.float32
FAR_Z = (4, 3, 5, 2, 6, 1, 7)
NT = (((1,), (1,)), ((), ()))
NN = (((1,), (0,)), ((), ()))


def dot(a, b, dims=NN):
    return lax.dot_general(a, b, dims, preferred_element_type=F32)


def split(x):
    hi = x.astype(BF)
    return hi, (x - hi.astype(F32)).astype(BF)


def dot3(ah, al, bh, bl, dims=NN):
    return dot(ah, bh, dims) + dot(ah, bl, dims) + dot(al, bh, dims)


def laplace(left_sq, right_sq, cross):
    dist_sq = jnp.maximum(left_sq + right_sq - 2.0 * cross, 1e-30)
    return jnp.exp(-(dist_sq * lax.rsqrt(dist_sq)))


def col_sq(x):
    sq = jnp.sum(jnp.square(x.astype(F32)), axis=1, keepdims=True)
    return jnp.broadcast_to(sq, (x.shape[0], 128))


def row_sq(x):
    hi, lo = split(jnp.square(x.astype(F32)))
    ones = jnp.ones((8, x.shape[1]), BF)
    return dot(ones, hi, NT) + dot(ones, lo, NT)


def widen(col, n):
    return jnp.concatenate([col] * (n // 128), axis=1)


def body(
    idx_ref, shr_ref, c_hbm, w_hbm, t_hbm, s_hbm, e_hbm, out_ref,
    c_v, w_v, t_v, e_v, e_pad, shr_pad,
    chosen, rsby, zsrc, rsbz, xsb, xrb, ball, sbuf, ebuf,
    wt, tt, c_col, b_row, s_row, kb,
    pred, rsp, xsp, xrp, rall, rhl, gbuf, mbuf, lacc,
    lsem, ss_yz, rs_yz, ss_m, rs_m,
):
    dp, ce = lax.axis_index("dp"), lax.axis_index("center")
    xlo, core = lax.div(dp, 2), lax.rem(dp, 2)
    y, xhi, z = lax.div(ce, 16), lax.rem(lax.div(ce, 8), 2), lax.rem(ce, 8)
    x = xhi * 2 + xlo
    chunk = y * NZ + z
    first = ce * ROWS

    def yz_peer(k):
        py = lax.rem(y + lax.div(k, NZ), NY)
        pz = lax.rem(z + lax.rem(k, NZ), NZ)
        return (dp, (py * NXH + xhi) * NZ + pz), py * NZ + pz

    def z_peer(j):
        return (dp, (y * NXH + xhi) * NZ + lax.rem(z + j, NZ))

    def y_peer(j):
        return (dp, (lax.rem(y + j, NY) * NXH + xhi) * NZ + z)

    def x_peer(j):
        px = lax.rem(x + j, NX)
        return (lax.rem(px, 2) * 2 + core, (y * NXH + lax.div(px, 2)) * NZ + z)

    sib = (xlo * 2 + 1 - core, ce)
    dpx = (1 - xlo) * 2 + core
    dps, dpxs = xlo * 2 + 1 - core, (1 - xlo) * 2 + 1 - core

    def slot(py, pz):
        return lax.rem(py, 2) * NZ + pz, slice(None), pl.ds(pl.multiple_of(lax.div(py, 2) * HALF, 128), HALF)

    lane = pl.ds(pl.multiple_of(core * HALF, 128), HALF)
    used, unsent = [], []

    def remote(src, dst, peer):
        slot = len(used)
        used.append(None)
        cp = pltpu.make_async_remote_copy(
            src_ref=src, dst_ref=dst, send_sem=ss_m.at[slot], recv_sem=rs_m.at[slot],
            device_id=peer, device_id_type=MESH,
        )
        cp.start()
        unsent.append(cp)
        return cp

    def drain(count=None):
        for cp in unsent[:count]:
            cp.wait_send()
        del unsent[:count]

    def yz_copy(phase, k, src, dst, peer):
        return pltpu.make_async_remote_copy(
            src_ref=src, dst_ref=dst, send_sem=ss_yz.at[phase, k - 1],
            recv_sem=rs_yz.at[phase, k - 1], device_id=peer, device_id_type=MESH,
        )

    def recv(copies):
        for cp in copies:
            cp.wait_recv()

    def local(i, src, dst):
        cp = pltpu.make_async_copy(src, dst, lsem.at[i])
        cp.start()
        return cp

    barrier = pltpu.get_barrier_semaphore()

    def greet(k, carry):
        pl.semaphore_signal(barrier, inc=1, device_id=yz_peer(NYZ - k)[0], device_id_type=MESH)
        return carry

    lax.fori_loop(1, NYZ, greet, 0)
    for j in range(1, NX):
        pl.semaphore_signal(barrier, inc=1, device_id=x_peer(j), device_id_type=MESH)
    pl.semaphore_signal(barrier, inc=1, device_id=sib, device_id_type=MESH)

    ld_c = local(0, c_hbm, c_v)
    ld_e = local(1, e_hbm, e_v)
    ld_s = local(
        2,
        s_hbm.at[pl.ds(pl.multiple_of(xlo * 16, 16), 16), lane],
        sbuf.at[x, y, z, :, lane],
    )
    ld_t = local(3, t_hbm, t_v)
    ld_w = local(4, w_hbm, w_v)

    e_pad[...] = jnp.zeros_like(e_pad)
    ld_e.wait()
    e_pad[:, :Q] = e_v[...]
    shr_pad[...] = jnp.zeros_like(shr_pad)
    shr_pad[0:1, :Q] = shr_ref[...]
    e_hi, e_lo = split(e_pad[pl.ds(pl.multiple_of(xlo * 16, 16), 16), :])
    ebuf[core, y, x, z] = jnp.where(core == 0, e_hi.astype(F32), e_lo.astype(F32)).astype(BF)
    idx_col = jnp.transpose(jnp.broadcast_to((idx_ref[...] - first).astype(F32), (128, BD)))
    ld_c.wait()
    chosen_f = jnp.zeros((BD, D), F32)
    for b in range(ROWS // 256):
        iota = lax.broadcasted_iota(jnp.int32, (BD, 256), 1).astype(F32) + float(b * 256)
        pick = jnp.where(widen(idx_col, 256) == iota, 1.0, 0.0).astype(BF)
        chosen_f += dot(pick, c_v[b * 256:(b + 1) * 256, :])
    chosen_b = chosen_f.astype(BF)
    chosen[...] = chosen_b.reshape(16, 16, D)
    ld_s.wait()
    pl.semaphore_wait(barrier, NYZ - 1 + NX)

    b_y = []
    for i, o in enumerate(FAR_Z + (0,)):
        pz = lax.rem(z + o, NZ)
        b_y.append([
            remote(chosen.at[slot(lax.rem(y + j, NY), pz)], rsby.at[i, j - 1], y_peer(j)) for j in range(1, NY)
        ])

    s_z = [remote(sbuf.at[x, y, z, :, lane], sbuf.at[x, y, z, :, lane], z_peer(o)) for o in FAR_Z]
    e_z = [remote(ebuf.at[core, y, x, z], ebuf.at[core, y, x, z], z_peer(o)) for o in FAR_Z]

    b_z = []
    for i, o in enumerate(FAR_Z + (0,)):
        recv(b_y[i])
        part_b = chosen[slot(y, lax.rem(z + o, NZ))].astype(F32)
        for j in range(NY - 1):
            part_b += rsby[i, j].astype(F32)
        if o:
            zsrc[i] = part_b.astype(BF)
            b_z.append(remote(zsrc.at[i], rsbz.at[i], z_peer(o)))
    recv(s_z)
    s_y = [remote(sbuf.at[x, y, :, :, lane], sbuf.at[x, y, :, :, lane], y_peer(j)) for j in range(1, NY)]
    recv(e_z)
    e_x = [remote(ebuf.at[core, y, x], ebuf.at[core, y, x], x_peer(j)) for j in range(1, NX)]
    for i in range(NZ - 1):
        recv([b_z[i]])
        part_b += rsbz[i].astype(F32)
    xsb[...] = part_b.astype(BF)
    b_x = remote(xsb, xrb, x_peer(2))
    ld_w.wait()

    def prep(b, carry):
        rows = pl.ds(pl.multiple_of(b * 256, 256), 256)
        hi, lo = split(jnp.transpose(w_v[rows, :]))
        wt[0, b] = hi
        wt[1, b] = lo
        c_col[rows, :] = col_sq(c_v[rows, :])
        return carry

    lax.fori_loop(0, ROWS // 256, prep, 0)
    ld_t.wait()
    tt[...] = jnp.transpose(t_v[...]).reshape(NYZ, 8, BD)

    recv([b_x])
    here = (dp,) + slot(y, z)
    ball[here] = (xsb[...].astype(F32) + xrb[...].astype(F32)).astype(BF)

    early = len(unsent)
    own = ball.at[here]
    g_z = {o: remote(own, own, z_peer(o)) for o in FAR_Z}
    g_y = [remote(own, own, y_peer(j)) for j in range(1, NY)]
    recv(s_y)
    s_x = [remote(sbuf.at[x, :, :, :, lane], sbuf.at[x, :, :, :, lane], x_peer(j)) for j in (1, 3)]
    s_s = [remote(sbuf.at[x, :, :, :, lane], sbuf.at[x, :, :, :, lane], sib)]
    for o in FAR_Z[::-1]:
        recv([g_z[o]])
        came = ball.at[(dp,) + slot(y, lax.rem(z + NZ - o, NZ))]
        g_y += [remote(came, came, y_peer(j)) for j in range(1, NY)]
    recv(e_x)
    e_y = [remote(ebuf.at[core, y], ebuf.at[core, y], y_peer(j)) for j in range(1, NY)]
    e_s = [remote(ebuf.at[core, y], ebuf.at[core, y], sib)]
    drain(early)
    recv(g_y)
    b_s = [remote(ball.at[dp], ball.at[dp], sib)]
    b_r = remote(ball.at[dp, pl.ds(0, 8)], ball.at[dp, pl.ds(0, 8)], x_peer(1))
    b_l = remote(ball.at[dp, pl.ds(8, 8)], ball.at[dp, pl.ds(8, 8)], x_peer(3))
    batch_sends = len(unsent)

    def norms_b(d):
        b_row[d] = row_sq(ball[d].reshape(BD, D))

    def k_rows(d, b, n):
        rows = pl.ds(pl.multiple_of(b * n, n), n)
        cross = dot(c_v[rows, :], ball[d].reshape(BD, D), NT)
        hi, lo = split(laplace(widen(c_col[rows, :], BD), b_row[d][0:1, :], cross))
        kb[0, d, rows, :] = hi
        kb[1, d, rows, :] = lo
        return hi, lo

    def k_block(d):
        norms_b(d)

        def step(b, carry):
            k_rows(d, b, 512)
            return carry

        lax.fori_loop(0, ROWS // 512, step, 0, unroll=True)

    norms_b(dp)
    pred[...] = jnp.zeros_like(pred)

    def pred_step(b, carry):
        kh, kl = k_rows(dp, b, 256)
        pred[...] += dot3(wt[0, b], wt[1, b], kh, kl).reshape(NYZ, 8, BD)
        return carry

    lax.fori_loop(0, ROWS // 256, pred_step, 0, unroll=True)

    def send_p(i, carry):
        k = NYZ - i
        peer, pc = yz_peer(k)
        yz_copy(0, k, pred.at[pc], rsp.at[k - 1], peer).start()
        return carry

    lax.fori_loop(1, NYZ, send_p, 0)
    recv(b_s)
    k_block(dps)
    recv(s_x)
    west = sbuf.at[lax.rem(x + 3, NX), :, :, :, lane]
    east = sbuf.at[lax.rem(x + 1, NX), :, :, :, lane]
    west_half = sbuf.at[lax.rem(x + 3, NX), pl.ds(0, 2), :, :, lane]
    east_half = sbuf.at[lax.rem(x + 1, NX), pl.ds(2, 2), :, :, lane]
    s_f = [remote(west_half, west_half, x_peer(1)), remote(east_half, east_half, x_peer(3))]
    s_s += [remote(west, west, sib), remote(east, east, sib)]
    recv([b_r, b_l])
    b_s2 = remote(ball.at[dpx], ball.at[dpx], sib)
    k_block(dpx)
    recv(e_y)
    e_s += [remote(ebuf.at[core, lax.rem(y + j, NY)], ebuf.at[core, lax.rem(y + j, NY)], sib) for j in range(1, NY)]
    drain(batch_sends)

    def subset_product(rows_b, left):
        n = rows_b.shape[0]
        acc = jnp.zeros((n, QP), F32)
        for xx in range(NX):
            for p in range(NY // 2):
                two = slice(2 * p, 2 * p + 2)
                cross = dot(rows_b, sbuf[xx, two].reshape(256, D), NT)
                kh, kl = split(laplace(widen(left, 256), s_row[xx][0:1, 256 * p:256 * p + 256], cross))
                acc += dot3(kh, kl, ebuf[0, two, xx].reshape(256, QP), ebuf[1, two, xx].reshape(256, QP))
        return acc

    def g_step(b):
        rows = pl.ds(pl.multiple_of(core * 1024 + b * 512, 512), 512)
        g = subset_product(c_v[rows, :], c_col[rows, :]) * -shr_pad[0:1, :]
        hi, lo = split(g)
        gbuf[0, rows, :] = hi
        gbuf[1, rows, :] = lo

    def add_p(k, acc):
        yz_copy(0, k, pred.at[0], rsp.at[k - 1], sib).wait_recv()
        return acc + rsp[k - 1]

    part_p = lax.fori_loop(1, NYZ, add_p, pred[chunk])
    xsp[...] = part_p
    p_x = remote(xsp, xrp, x_peer(2))
    recv([b_s2])
    k_block(dpxs)
    recv(s_f)
    s_s += [remote(sbuf.at[lax.rem(x + 2, NX), :, :, :, lane], sbuf.at[lax.rem(x + 2, NX), :, :, :, lane], sib)]

    def sent_p(k, carry):
        yz_copy(0, k, pred.at[0], rsp.at[0], sib).wait_send()
        return carry

    lax.fori_loop(1, NYZ, sent_p, 0)
    recv([p_x])
    rall[dp, chunk] = xsp[...] + xrp[...] - tt[chunk]

    def send_r(i, carry):
        k = NYZ - i
        peer, pc = yz_peer(k)
        yz_copy(1, k, rall.at[dp, chunk], rall.at[dp, chunk], peer).start()
        return carry

    lax.fori_loop(1, NYZ, send_r, 0)
    recv(e_s + s_s)
    for xx in range(NX):
        s_row[xx] = row_sq(sbuf[xx].reshape(512, D))
    b_part = ball[core * 2 + lax.div(y, 2), pl.ds(lax.rem(y, 2) * 8, 8)].reshape(128, D)
    m_mine = pl.ds(pl.multiple_of(core * 512 + y * 128, 128), 128)
    m_hi, m_lo = split(subset_product(b_part, col_sq(b_part)))
    mbuf[0, m_mine, :] = m_hi
    mbuf[1, m_mine, :] = m_lo
    m_y = [remote(mbuf.at[:, m_mine], mbuf.at[:, m_mine], y_peer(j)) for j in range(1, NY)]
    g_step(0)

    def got_r(k, carry):
        yz_copy(1, k, rall.at[dp, chunk], rall.at[dp, chunk], sib).wait_recv()
        return carry

    r_x = {}
    for j in (0, 1, 3, 2):
        lax.fori_loop(max(1, j * NZ), (j + 1) * NZ, got_r, 0)
        line_y = lax.rem(y + NY - j, NY)
        line = rall.at[dp, pl.ds(pl.multiple_of(line_y * NZ, NZ), NZ)]
        r_x[j] = remote(line, line, x_peer(1 + 2 * lax.div(line_y, 2)))
    r_s = remote(rall.at[dp], rall.at[dp], sib)
    g_step(1)
    g_rows = pl.ds(pl.multiple_of(core * 1024, 1024), 1024)
    gm_s = [remote(gbuf.at[:, g_rows], gbuf.at[:, g_rows], sib)]

    def sent_r(k, carry):
        yz_copy(1, k, rall.at[0, 0], rall.at[0, 0], sib).wait_send()
        return carry

    lax.fori_loop(1, NYZ, sent_r, 0)
    r_s2 = []
    for j in (0, 1, 3, 2):
        recv([r_x[j]])
        line = rall.at[dpx, pl.ds(pl.multiple_of(lax.rem(y + NY - j, NY) * NZ, NZ), NZ)]
        r_s2.append(remote(line, line, sib))
    recv(m_y)
    m_rows = pl.ds(pl.multiple_of(core * 512, 512), 512)
    gm_s += [remote(mbuf.at[:, m_rows], mbuf.at[:, m_rows], sib)]

    def split_r(d):
        hi, lo = split(rall[d].reshape(OUTS, BD) * (1.0 / BATCH**0.5))
        rhl[0, d] = hi
        rhl[1, d] = lo

    def k_out(rows, d):
        return dot3(kb[0, d, rows, :], kb[1, d, rows, :], rhl[0, d], rhl[1, d], NT)

    def lift_t(d):
        rows = pl.ds(pl.multiple_of(d * BD, BD), BD)
        return dot3(rhl[0, d], rhl[1, d], mbuf[0, rows, :], mbuf[1, rows, :])

    recv([r_s])
    split_r(dp)
    split_r(dps)

    def out_near(b, carry):
        rows = pl.ds(pl.multiple_of(b * 256, 256), 256)
        out_ref[rows, :] = k_out(rows, dp) + k_out(rows, dps)
        return carry

    lax.fori_loop(0, ROWS // 256, out_near, 0, unroll=True)
    recv(r_s2)
    split_r(dpx)
    split_r(dpxs)
    recv(gm_s)
    lacc[...] = lift_t(0) + lift_t(1) + lift_t(2) + lift_t(3)
    l_hi, l_lo = split(lacc[...])

    def out_far(b, carry):
        rows = pl.ds(pl.multiple_of(b * 256, 256), 256)
        corr = dot3(gbuf[0, rows, :], gbuf[1, rows, :], l_hi, l_lo, NT)
        out_ref[rows, :] += k_out(rows, dpx) + k_out(rows, dpxs) + corr
        return carry

    lax.fori_loop(0, ROWS // 256, out_far, 0, unroll=True)
    drain()


N_MISC = 144


def shards(centers, weights, batch_index, targets, subset_points, eigvecs, shrink):
    v = pltpu.VMEM
    any_spec = pl.BlockSpec(memory_space=pl.ANY)
    vm = pl.BlockSpec(memory_space=pltpu.VMEM)
    return pl.pallas_call(
        body,
        out_shape=pltpu.VMEM((ROWS, OUTS), F32),
        in_specs=[vm, vm] + [any_spec] * 5,
        out_specs=vm,
        scratch_shapes=[
            v((ROWS, D), BF), v((ROWS, OUTS), F32), v((BD, OUTS), F32), v((32, Q), F32), v((32, QP), F32), v((8, QP), F32),
            v((16, 16, D), BF), v((NZ, NY - 1, 16, HALF), BF), v((NZ - 1, 16, HALF), BF), v((NZ - 1, 16, HALF), BF), v((16, HALF), BF), v((16, HALF), BF), v((4, 16, 16, D), BF),
            v((NX, NY, NZ, 16, D), BF), v((2, NY, NX, NZ, 16, QP), BF),
            v((2, ROWS // 256, OUTS, 256), BF), v((NYZ, 8, BD), F32), v((ROWS, 128), F32), v((4, 8, BD), F32), v((NX, 8, 512), F32), v((2, 4, ROWS, BD), BF),
            v((NYZ, 8, BD), F32), v((NYZ - 1, 8, BD), F32), v((8, BD), F32), v((8, BD), F32), v((4, NYZ, 8, BD), F32), v((2, 4, OUTS, BD), BF),
            v((2, ROWS, QP), BF), v((2, BATCH, QP), BF), v((OUTS, QP), F32),
            pltpu.SemaphoreType.DMA((5,)),
            pltpu.SemaphoreType.DMA((2, NYZ - 1)), pltpu.SemaphoreType.DMA((2, NYZ - 1)),
            pltpu.SemaphoreType.DMA((N_MISC,)), pltpu.SemaphoreType.DMA((N_MISC,)),
        ],
        compiler_params=pltpu.CompilerParams(collective_id=0, has_side_effects=True, vmem_limit_bytes=56 * 2**20),
        name="eigenpro_step",
    )(batch_index.reshape(1, BD), shrink.reshape(1, Q), centers, weights, targets, subset_points, eigvecs)


def solution(mesh):
    return jax.shard_map(
        shards,
        mesh=mesh,
        in_specs=(
            P("center", None),
            P("center", None),
            P("dp"),
            P("dp", None),
            P("center", None),
            P("center", None),
            P(),
        ),
        out_specs=P("center", None),
        check_vma=False,
    )
```
